32 devices in a mesh: row: 4 (over y, x), blk: 8 (over z, core).
Axes of the slice: x: 2, y: 2, z: 4, core: 2. Of those that a mesh axis runs over, the one named last changes fastest.
Arguments:
- grad: bfloat16 [4, 1024, 4096], P(None, 'row', 'blk'), may hold values from -6 to 6
- exp_avg: float32 [4, 1024, 4096], P(None, 'row', 'blk'), may hold values from -6 to 6
- exp_avg_sq: float32 [4, 1024, 4096], P(None, 'row', 'blk'), may hold values from 0.1 to 4
- left_basis: bfloat16 [4, 1024, 1024], P(None, 'row', 'blk'), may hold values from -0.1875 to 0.1875
- right_basis: bfloat16 [4096, 1024], P('blk', 'row'), may hold values from -0.1875 to 0.1875
Outputs:
- update: bfloat16 [4, 1024, 4096], P(None, 'row', 'blk')
- moment: float32 [4, 1024, 4096], P(None, 'row', 'blk')
- variance: float32 [4, 1024, 4096], P(None, 'row', 'blk')
The draws below stay inside these ranges and needn't reach their ends.
All inputs are finite; a program needn't handle non-finite values.
Results may differ from the reference program's by a relative error of at most 0.0061.
Values may be sent and summed in bfloat16 or wider, within the bound.
A program may use at most 128 MiB of HBM per device.

```python
import math
import jax
import jax.numpy as jnp
from jax import lax

B = 1024
NL = 4
C = 4096


def block_scale(own_key, shape, cuts, smallest, top_value):
    gain = 1.0
    for dim, blocks in cuts:
        steps = jax.random.uniform(jax.random.fold_in(jax.random.fold_in(own_key, 6), dim), (blocks,), jnp.float32, smallest / len(cuts), top_value / len(cuts))
        gain = gain * jnp.repeat(jnp.exp(steps), shape[dim] // blocks).reshape((-1,) + (1,) * (len(shape) - 1 - dim))
    return gain


def bell_draw(rng, dims, deviation, reach, cuts=(), held_as=jnp.bfloat16):
    loudness = block_scale(rng, dims, cuts, -0.22, 0.18) if cuts else 1.0
    entries = jax.random.normal(rng, dims, jnp.float32) * deviation * loudness
    return jnp.minimum(jnp.maximum(entries, -reach), reach).astype(held_as)


def setup_inputs(seed: int = 0) -> dict:
    seeds = jax.random.split(jax.random.key(seed), 6)
    grad = bell_draw(seeds[0], (NL, B, C), 1.0, 6.0, ((1, 4), (2, 8)))
    exp_avg = bell_draw(seeds[1], (NL, B, C), 1.0, 6.0, ((1, 4), (2, 8)), jnp.float32)
    exp_avg_sq = jnp.clip(jnp.exp(math.log(4.0) - 3.6888794 * jax.random.uniform(seeds[2], (NL, B, C), jnp.float32) ** block_scale(seeds[2], (NL, B, C), ((1, 4), (2, 8)), -0.2, 0.2)), 0.1, 4.0)
    left_basis = bell_draw(seeds[3], (NL, B, B), B ** -0.5, 0.1875, ((1, 4), (2, 8)))
    right_basis = bell_draw(seeds[4], (C, B), B ** -0.5, 0.1875, ((0, 8), (1, 4)))
    return dict(grad=grad, exp_avg=exp_avg, exp_avg_sq=exp_avg_sq, left_basis=left_basis, right_basis=right_basis)


momentum_decay = 0.9
variance_decay = 0.95
epsilon_value = 1e-08

def reference(grad, exp_avg, exp_avg_sq, left_basis, right_basis):
    high = lax.Precision.HIGHEST
    moment = momentum_decay * exp_avg + (1.0 - momentum_decay) * grad.astype(jnp.float32)
    moment_half = moment.astype(jnp.bfloat16)
    left = left_basis.astype(jnp.float32)
    right = right_basis.astype(jnp.float32).reshape(C // B, B, B)

    def rotate_in(data):
        lefted = jnp.einsum('ikn,ikc->inc', left, data.astype(jnp.float32), precision=high).astype(jnp.bfloat16)
        flat = lefted.astype(jnp.float32).reshape(NL * B, C // B, B)
        return jnp.einsum('rjk,jkn->rjn', flat, right, precision=high).reshape(NL, B, C)
    grad_rot = rotate_in(grad)
    moment_rot = rotate_in(moment_half)
    variance = variance_decay * exp_avg_sq + (1.0 - variance_decay) * grad_rot * grad_rot
    direction = (moment_rot / (jnp.sqrt(variance) + epsilon_value)).astype(jnp.bfloat16)
    flat = direction.astype(jnp.float32).reshape(NL * B, C // B, B)
    back = jnp.einsum('rjn,jkn->rjk', flat, right, precision=high).reshape(NL, B, C).astype(jnp.bfloat16)
    update = jnp.einsum('ink,ikc->inc', left, back.astype(jnp.float32), precision=high).astype(jnp.bfloat16)
    return (update, moment, variance)
```

```python
import functools

import jax
import jax.numpy as jnp
from jax import lax
from jax.experimental import pallas as pl
from jax.experimental.pallas import tpu as pltpu
from jax.sharding import PartitionSpec as P

momentum_decay = 0.9
variance_decay = 0.95
epsilon_value = 1e-08


def from_partner(value, axis, bit):
    mask = 2**bit
    pairs = [(source, source ^ mask) for source in range(lax.axis_size(axis))]
    return lax.ppermute(value, axis, pairs)


def spread_block(data, groups):
    blocks, brows, cols = data.shape
    narrow = cols // groups
    return (
        data.reshape(blocks, brows, groups, narrow)
        .transpose(0, 2, 1, 3)
        .reshape(blocks * groups, brows, narrow)
    )


def join_block(data, blocks, groups):
    total, brows, narrow = data.shape
    return (
        data.reshape(blocks, groups, brows, narrow)
        .transpose(0, 2, 1, 3)
        .reshape(blocks, brows, groups * narrow)
    )


def general_body(grad, exp_avg, exp_avg_sq, left_basis, right_basis):
    blocks, brows, cols = grad.shape
    moment = momentum_decay * exp_avg + (1.0 - momentum_decay) * grad.astype(jnp.float32)
    moment_half = moment.astype(jnp.bfloat16)
    left_rows = lax.all_gather(left_basis, "blk", axis=2, tiled=True)
    right_rows = lax.all_gather(right_basis, "row", axis=1, tiled=True)
    groups = lax.axis_size("row") // blocks
    grad_group, moment_group = (
        lax.all_to_all(spread_block(grad, groups), "row", split_axis=0, concat_axis=1, tiled=True),
        lax.all_to_all(
            spread_block(moment_half, groups), "row", split_axis=0, concat_axis=1, tiled=True
        ),
    )
    picked = jnp.repeat(left_rows, groups, axis=0)
    block_rows = lax.all_to_all(picked, "row", split_axis=0, concat_axis=0, tiled=True)
    own_block = block_rows.reshape(block_rows.shape[0] * brows, block_rows.shape[2])
    grad_turned = jnp.einsum(
        "kn,kc->nc", own_block, grad_group[0], preferred_element_type=jnp.float32
    ).astype(jnp.bfloat16)
    moment_turned = jnp.einsum(
        "kn,kc->nc", own_block, moment_group[0], preferred_element_type=jnp.float32
    ).astype(jnp.bfloat16)
    grad_back, moment_back = (
        lax.all_to_all(grad_turned[None], "row", split_axis=1, concat_axis=0, tiled=True),
        lax.all_to_all(moment_turned[None], "row", split_axis=1, concat_axis=0, tiled=True),
    )
    grad_left = join_block(grad_back, blocks, groups)
    moment_left = join_block(moment_back, blocks, groups)
    half = lax.axis_index("blk") % 2
    grad_term = jnp.dot(
        grad_left.reshape(blocks * brows, cols), right_rows, preferred_element_type=jnp.float32
    )
    moment_term = jnp.dot(
        moment_left.reshape(blocks * brows, cols), right_rows, preferred_element_type=jnp.float32
    )
    own_start = half * cols
    other_start = (1 - half) * cols
    grad_other, moment_other = from_partner(
        (
            lax.dynamic_slice_in_dim(grad_term, other_start, cols, 1),
            lax.dynamic_slice_in_dim(moment_term, other_start, cols, 1),
        ),
        "blk",
        0,
    )
    grad_rot = lax.dynamic_slice_in_dim(grad_term, own_start, cols, 1) + grad_other
    moment_rot = lax.dynamic_slice_in_dim(moment_term, own_start, cols, 1) + moment_other
    variance = (
        variance_decay * exp_avg_sq.reshape(blocks * brows, cols)
        + (1.0 - variance_decay) * grad_rot * grad_rot
    )
    direction = (moment_rot / (jnp.sqrt(variance) + epsilon_value)).astype(jnp.bfloat16)
    partner_dir = from_partner(direction, "blk", 0)
    own_rows = lax.dynamic_slice_in_dim(right_rows, own_start, cols, 1)
    other_rows = lax.dynamic_slice_in_dim(right_rows, other_start, cols, 1)
    contract = (((1,), (1,)), ((), ()))
    back = lax.dot_general(direction, own_rows, contract, preferred_element_type=jnp.float32)
    back = back + lax.dot_general(
        partner_dir, other_rows, contract, preferred_element_type=jnp.float32
    )
    back = back.astype(jnp.bfloat16).reshape(blocks, brows, cols)
    back_group = lax.all_to_all(
        spread_block(back, groups), "row", split_axis=0, concat_axis=1, tiled=True
    )
    result = jnp.einsum(
        "nk,kc->nc", own_block, back_group[0], preferred_element_type=jnp.float32
    ).astype(jnp.bfloat16)
    update = join_block(
        lax.all_to_all(result[None], "row", split_axis=1, concat_axis=0, tiled=True), blocks, groups
    )
    return (update, moment, variance.reshape(blocks, brows, cols))


def kernel(
    nrow,
    nblk,
    grad,
    exp_avg,
    exp_avg_sq,
    left,
    right,
    rot_out,
    update_out,
    grad_own,
    avg_own,
    sq_own,
    moment_half,
    sq_half,
    gathered,
    sq_all,
    basis,
    turn,
    turn_other,
    turned,
    turned_other,
    grad_rot,
    moment_rot,
    rot_half,
    direction,
    direction_other,
    back,
    update,
    send_sems,
    recv_sems,
    local_sems,
):
    brows, cols = grad.shape[1], grad.shape[2]
    width = left.shape[2]
    narrow = right.shape[1]
    row = lax.axis_index("row")
    blk = lax.axis_index("blk")
    core = lax.rem(blk, 2)
    partner = blk + 1 - 2 * core
    counter = [0, 0]

    def at_row(step):
        return lax.rem(row + step, nrow)

    def at_blk(step):
        return lax.rem(blk + 2 * step, nblk)

    def rows_of(index):
        return pl.ds(pl.multiple_of(index * brows, brows), brows)

    def lanes_of(index):
        return pl.ds(pl.multiple_of(index * width, width), width)

    def remote(source, target, to_row, to_blk):
        index = counter[0]
        counter[0] += 1
        copy = pltpu.make_async_remote_copy(
            src_ref=source,
            dst_ref=target,
            send_sem=send_sems.at[index],
            recv_sem=recv_sems.at[index],
            device_id=(to_row, to_blk),
            device_id_type=pl.DeviceIdType.MESH,
        )
        copy.start()
        return copy

    def local(source, target):
        index = counter[1]
        counter[1] += 1
        copy = pltpu.make_async_copy(source, target, local_sems.at[index])
        copy.start()
        return copy

    load_grad = local(grad, grad_own)
    load_avg = local(exp_avg, avg_own)
    load_left = local(left.at[row], basis.at[rows_of(row), lanes_of(blk)])
    load_block = local(grad.at[row], gathered.at[rows_of(row), pl.ds(0, cols)])
    load_sq = local(exp_avg_sq, sq_own)

    def right_place(source_row):
        slot = lax.rem(source_row // (nrow // 2) + core, 2)
        start = lax.rem(source_row, nrow // 2) * narrow
        return turn.at[slot, :, pl.ds(pl.multiple_of(start, narrow), narrow)]

    load_right = local(right, right_place(row))

    barrier = pltpu.get_barrier_semaphore()
    peers = [(at_row(step), blk) for step in range(1, nrow)]
    peers += [(row, at_blk(step)) for step in range(1, nblk // 2)]
    peers += [(row, partner)]
    for peer in peers:
        pl.semaphore_signal(barrier, inc=1, device_id=peer, device_id_type=pl.DeviceIdType.MESH)
    pl.semaphore_wait(barrier, len(peers))

    sent = []
    left_copies = [
        remote(left.at[at_row(step)], basis.at[rows_of(row), lanes_of(blk)], at_row(step), blk)
        for step in range(1, nrow)
    ]
    grad_copies = [
        remote(
            grad.at[at_row(step)], gathered.at[rows_of(row), pl.ds(0, cols)], at_row(step), blk
        )
        for step in range(1, nrow)
    ]
    load_grad.wait()
    load_avg.wait()
    moment_copies = []
    for step in list(range(1, nrow)) + [0]:
        index = at_row(step)
        moment = momentum_decay * avg_own[index] + (1.0 - momentum_decay) * grad_own[
            index
        ].astype(jnp.float32)
        if step == 0:
            gathered[rows_of(row), cols:] = moment.astype(jnp.bfloat16)
        else:
            moment_half[index] = moment.astype(jnp.bfloat16)
            moment_copies.append(
                remote(
                    moment_half.at[index],
                    gathered.at[rows_of(row), pl.ds(cols, cols)],
                    index,
                    blk,
                )
            )
    right_copies = [
        remote(right, right_place(row), at_row(step), blk) for step in range(1, nrow)
    ]

    load_left.wait()
    for copy in left_copies:
        copy.wait_recv()
    own_lanes = basis.at[:, lanes_of(blk)]
    spread_copies = [
        remote(own_lanes, own_lanes, row, at_blk(step)) for step in range(1, nblk // 2)
    ]
    share_copies = [remote(own_lanes, own_lanes, row, partner)]

    load_sq.wait()
    sq_copies = []
    for step in list(range(1, nrow)) + [0]:
        index = at_row(step)
        value = sq_own[index].astype(jnp.bfloat16)
        if step == 0:
            sq_all[rows_of(row), :] = value
        else:
            sq_half[index] = value

    for step in range(1, nblk // 2):
        spread_copies[step - 1].wait_recv()
        lanes = basis.at[:, lanes_of(at_blk(nblk // 2 - step))]
        share_copies.append(remote(lanes, lanes, row, partner))

    for step in range(1, nrow):
        index = at_row(step)
        sq_copies.append(remote(sq_half.at[index], sq_all.at[rows_of(row), :], index, blk))

    load_right.wait()
    for copy in right_copies:
        copy.wait_recv()
    turn_copy = remote(turn.at[1], turn_other, row, partner)

    load_block.wait()
    for copy in share_copies + grad_copies + moment_copies:
        copy.wait_recv()

    turned_copies = []
    for index in range(nrow):
        part = pl.ds(index * brows, brows)
        turned[part, :] = lax.dot_general(
            basis[:, part],
            gathered[...],
            (((0,), (0,)), ((), ())),
            preferred_element_type=jnp.float32,
        ).astype(jnp.bfloat16)
        turned_copies.append(remote(turned.at[part, :], turned_other.at[part, :], row, partner))

    turn_copy.wait_recv()
    for copy in turned_copies:
        copy.wait_recv()
    rot_copies = []
    order = list(range(1, nrow)) + [0]
    for step in order:
        index = at_row(step)
        part = rows_of(index)
        grad_term = jnp.dot(turned[part, :cols], turn[0], preferred_element_type=jnp.float32)
        grad_term += jnp.dot(
            turned_other[part, :cols], turn_other[...], preferred_element_type=jnp.float32
        )
        grad_rot[part, :] = grad_term
        rot_half[part, :] = grad_term.astype(jnp.bfloat16)
        if step == 0:
            rot_local = local(rot_half.at[part, :], rot_out.at[row])
        else:
            rot_copies.append(remote(rot_half.at[part, :], rot_out.at[row], index, blk))
    for step in order:
        part = rows_of(at_row(step))
        moment_term = jnp.dot(turned[part, cols:], turn[0], preferred_element_type=jnp.float32)
        moment_term += jnp.dot(
            turned_other[part, cols:], turn_other[...], preferred_element_type=jnp.float32
        )
        moment_rot[part, :] = moment_term

    direction_copies = []
    for step in range(nrow):
        index = at_row(nrow - step)
        part = rows_of(index)
        if step:
            sq_copies[step - 1].wait_recv()
        rotated = grad_rot[part, :]
        variance = (
            variance_decay * sq_all[part, :].astype(jnp.float32)
            + (1.0 - variance_decay) * rotated * rotated
        )
        direction[part, :] = (
            moment_rot[part, :] / (jnp.sqrt(variance) + epsilon_value)
        ).astype(jnp.bfloat16)
        direction_copies.append(
            remote(direction.at[part, :], direction_other.at[part, :], row, partner)
        )

    contract = (((1,), (1,)), ((), ()))
    for step in range(nrow):
        part = rows_of(at_row(nrow - step))
        direction_copies[step].wait_recv()
        term = lax.dot_general(
            direction[part, :], turn[0], contract, preferred_element_type=jnp.float32
        )
        term += lax.dot_general(
            direction_other[part, :], turn[1], contract, preferred_element_type=jnp.float32
        )
        back[part, :] = term.astype(jnp.bfloat16)

    update_copies = []
    for step in order:
        index = at_row(step)
        part = rows_of(index)
        update[part, :] = jnp.dot(
            basis[part, :], back[...], preferred_element_type=jnp.float32
        ).astype(jnp.bfloat16)
        if step == 0:
            update_local = local(update.at[part, :], update_out.at[row])
        else:
            update_copies.append(remote(update.at[part, :], update_out.at[row], index, blk))

    rot_local.wait()
    update_local.wait()
    for copy in rot_copies + update_copies:
        copy.wait_recv()
    for copy in (
        left_copies
        + grad_copies
        + moment_copies
        + right_copies
        + spread_copies
        + share_copies
        + sq_copies
        + [turn_copy]
        + turned_copies
        + rot_copies
        + direction_copies
        + update_copies
    ):
        copy.wait_send()


def fast_body(grad, exp_avg, exp_avg_sq, left_basis, right_basis):
    blocks, brows, cols = grad.shape
    nrow, nblk = lax.axis_size("row"), lax.axis_size("blk")
    size = nrow * brows
    half, full = jnp.bfloat16, jnp.float32
    vmem = pltpu.VMEM
    remote_count = 7 * (nrow - 1) + 2 * (nblk // 2 - 1) + 2 + 2 * nrow
    rot, update = pl.pallas_call(
        functools.partial(kernel, nrow, nblk),
        out_shape=[jax.ShapeDtypeStruct(grad.shape, half)] * 2,
        in_specs=[pl.BlockSpec(memory_space=pl.ANY)] * 5,
        out_specs=[pl.BlockSpec(memory_space=pl.ANY)] * 2,
        scratch_shapes=[
            vmem(grad.shape, half),
            vmem(grad.shape, full),
            vmem(grad.shape, full),
            vmem(grad.shape, half),
            vmem(grad.shape, half),
            vmem((size, 2 * cols), half),
            vmem((size, cols), half),
            vmem((size, size), half),
            vmem((2, cols, cols), half),
            vmem((cols, cols), half),
            vmem((size, 2 * cols), half),
            vmem((size, 2 * cols), half),
            vmem((size, cols), full),
            vmem((size, cols), full),
            vmem((size, cols), half),
            vmem((size, cols), half),
            vmem((size, cols), half),
            vmem((size, cols), half),
            vmem((size, cols), half),
            pltpu.SemaphoreType.DMA((remote_count,)),
            pltpu.SemaphoreType.DMA((remote_count,)),
            pltpu.SemaphoreType.DMA((8,)),
        ],
        compiler_params=pltpu.CompilerParams(
            collective_id=0, has_side_effects=True, vmem_limit_bytes=56 * 2**20
        ),
        cost_estimate=pl.CostEstimate(
            flops=12 * size * size * cols, bytes_accessed=16 * size * cols, transcendentals=0
        ),
    )(grad, exp_avg, exp_avg_sq, left_basis, right_basis)
    moment = momentum_decay * exp_avg + (1.0 - momentum_decay) * grad.astype(full)
    rotated = rot.astype(full)
    variance = variance_decay * exp_avg_sq + (1.0 - variance_decay) * rotated * rotated
    return (update, moment, variance)


def body(grad, exp_avg, exp_avg_sq, left_basis, right_basis):
    blocks, brows, cols = grad.shape
    nrow, nblk = lax.axis_size("row"), lax.axis_size("blk")
    size = nrow * brows
    fits = (
        blocks == nrow
        and nrow % 2 == 0
        and nblk * left_basis.shape[2] == size
        and size == 2 * cols
        and left_basis.shape[2] % 128 == 0
        and right_basis.shape[0] == cols
        and right_basis.shape[1] * nrow == size
        and right_basis.shape[1] % 128 == 0
        and brows % 128 == 0
    )
    run = fast_body if fits else general_body
    return run(grad, exp_avg, exp_avg_sq, left_basis, right_basis)


def solution(mesh):
    in_specs = (
        P(None, "row", "blk"),
        P(None, "row", "blk"),
        P(None, "row", "blk"),
        P(None, "row", "blk"),
        P("blk", "row"),
    )
    out_specs = (P(None, "row", "blk"), P(None, "row", "blk"), P(None, "row", "blk"))
    return jax.shard_map(body, mesh=mesh, in_specs=in_specs, out_specs=out_specs, check_vma=False)
```

```python
import functools

import jax
import jax.numpy as jnp
from jax import lax
from jax.experimental import pallas as pl
from jax.experimental.pallas import tpu as pltpu
from jax.sharding import PartitionSpec as P

momentum_decay = 0.9
variance_decay = 0.95
epsilon_value = 1e-08


def from_partner(value, axis, bit):
    mask = 2**bit
    pairs = [(source, source ^ mask) for source in range(lax.axis_size(axis))]
    return lax.ppermute(value, axis, pairs)


def spread_block(data, groups):
    blocks, brows, cols = data.shape
    narrow = cols // groups
    return (
        data.reshape(blocks, brows, groups, narrow)
        .transpose(0, 2, 1, 3)
        .reshape(blocks * groups, brows, narrow)
    )


def join_block(data, blocks, groups):
    total, brows, narrow = data.shape
    return (
        data.reshape(blocks, groups, brows, narrow)
        .transpose(0, 2, 1, 3)
        .reshape(blocks, brows, groups * narrow)
    )


def general_body(grad, exp_avg, exp_avg_sq, left_basis, right_basis):
    blocks, brows, cols = grad.shape
    moment = momentum_decay * exp_avg + (1.0 - momentum_decay) * grad.astype(jnp.float32)
    moment_half = moment.astype(jnp.bfloat16)
    left_rows = lax.all_gather(left_basis, "blk", axis=2, tiled=True)
    right_rows = lax.all_gather(right_basis, "row", axis=1, tiled=True)
    groups = lax.axis_size("row") // blocks
    grad_group, moment_group = (
        lax.all_to_all(spread_block(grad, groups), "row", split_axis=0, concat_axis=1, tiled=True),
        lax.all_to_all(
            spread_block(moment_half, groups), "row", split_axis=0, concat_axis=1, tiled=True
        ),
    )
    picked = jnp.repeat(left_rows, groups, axis=0)
    block_rows = lax.all_to_all(picked, "row", split_axis=0, concat_axis=0, tiled=True)
    own_block = block_rows.reshape(block_rows.shape[0] * brows, block_rows.shape[2])
    grad_turned = jnp.einsum(
        "kn,kc->nc", own_block, grad_group[0], preferred_element_type=jnp.float32
    ).astype(jnp.bfloat16)
    moment_turned = jnp.einsum(
        "kn,kc->nc", own_block, moment_group[0], preferred_element_type=jnp.float32
    ).astype(jnp.bfloat16)
    grad_back, moment_back = (
        lax.all_to_all(grad_turned[None], "row", split_axis=1, concat_axis=0, tiled=True),
        lax.all_to_all(moment_turned[None], "row", split_axis=1, concat_axis=0, tiled=True),
    )
    grad_left = join_block(grad_back, blocks, groups)
    moment_left = join_block(moment_back, blocks, groups)
    half = lax.axis_index("blk") % 2
    grad_term = jnp.dot(
        grad_left.reshape(blocks * brows, cols), right_rows, preferred_element_type=jnp.float32
    )
    moment_term = jnp.dot(
        moment_left.reshape(blocks * brows, cols), right_rows, preferred_element_type=jnp.float32
    )
    own_start = half * cols
    other_start = (1 - half) * cols
    grad_other, moment_other = from_partner(
        (
            lax.dynamic_slice_in_dim(grad_term, other_start, cols, 1),
            lax.dynamic_slice_in_dim(moment_term, other_start, cols, 1),
        ),
        "blk",
        0,
    )
    grad_rot = lax.dynamic_slice_in_dim(grad_term, own_start, cols, 1) + grad_other
    moment_rot = lax.dynamic_slice_in_dim(moment_term, own_start, cols, 1) + moment_other
    variance = (
        variance_decay * exp_avg_sq.reshape(blocks * brows, cols)
        + (1.0 - variance_decay) * grad_rot * grad_rot
    )
    direction = (moment_rot / (jnp.sqrt(variance) + epsilon_value)).astype(jnp.bfloat16)
    partner_dir = from_partner(direction, "blk", 0)
    own_rows = lax.dynamic_slice_in_dim(right_rows, own_start, cols, 1)
    other_rows = lax.dynamic_slice_in_dim(right_rows, other_start, cols, 1)
    contract = (((1,), (1,)), ((), ()))
    back = lax.dot_general(direction, own_rows, contract, preferred_element_type=jnp.float32)
    back = back + lax.dot_general(
        partner_dir, other_rows, contract, preferred_element_type=jnp.float32
    )
    back = back.astype(jnp.bfloat16).reshape(blocks, brows, cols)
    back_group = lax.all_to_all(
        spread_block(back, groups), "row", split_axis=0, concat_axis=1, tiled=True
    )
    result = jnp.einsum(
        "nk,kc->nc", own_block, back_group[0], preferred_element_type=jnp.float32
    ).astype(jnp.bfloat16)
    update = join_block(
        lax.all_to_all(result[None], "row", split_axis=1, concat_axis=0, tiled=True), blocks, groups
    )
    return (update, moment, variance.reshape(blocks, brows, cols))


def kernel(
    nrow,
    nblk,
    grad,
    exp_avg,
    exp_avg_sq,
    left,
    right,
    update_out,
    moment_out,
    variance_out,
    rot_out,
    grad_own,
    avg_own,
    sq_own,
    moment_half,
    sq_half,
    gathered,
    sq_all,
    basis,
    turn,
    turn_other,
    turned,
    turned_other,
    grad_rot,
    moment_rot,
    rot_half,
    direction,
    direction_other,
    back,
    update,
    send_sems,
    recv_sems,
    local_sems,
):
    brows, cols = grad.shape[1], grad.shape[2]
    width = left.shape[2]
    narrow = right.shape[1]
    row = lax.axis_index("row")
    blk = lax.axis_index("blk")
    core = lax.rem(blk, 2)
    partner = blk + 1 - 2 * core
    counter = [0, 0]

    def at_row(step):
        return lax.rem(row + step, nrow)

    def at_blk(step):
        return lax.rem(blk + 2 * step, nblk)

    def rows_of(index):
        return pl.ds(pl.multiple_of(index * brows, brows), brows)

    def lanes_of(index):
        return pl.ds(pl.multiple_of(index * width, width), width)

    def remote(source, target, to_row, to_blk):
        index = counter[0]
        counter[0] += 1
        copy = pltpu.make_async_remote_copy(
            src_ref=source,
            dst_ref=target,
            send_sem=send_sems.at[index],
            recv_sem=recv_sems.at[index],
            device_id=(to_row, to_blk),
            device_id_type=pl.DeviceIdType.MESH,
        )
        copy.start()
        return copy

    def local(source, target):
        index = counter[1]
        counter[1] += 1
        copy = pltpu.make_async_copy(source, target, local_sems.at[index])
        copy.start()
        return copy

    load_grad = local(grad, grad_own)
    load_avg = local(exp_avg, avg_own)
    load_left = local(left.at[row], basis.at[rows_of(row), lanes_of(blk)])
    load_block = local(grad.at[row], gathered.at[rows_of(row), pl.ds(0, cols)])
    load_sq = local(exp_avg_sq, sq_own)

    def right_place(source_row):
        slot = lax.rem(source_row // (nrow // 2) + core, 2)
        start = lax.rem(source_row, nrow // 2) * narrow
        return turn.at[slot, :, pl.ds(pl.multiple_of(start, narrow), narrow)]

    load_right = local(right, right_place(row))

    barrier = pltpu.get_barrier_semaphore()
    peers = [(at_row(step), blk) for step in range(1, nrow)]
    peers += [(row, at_blk(step)) for step in range(1, nblk // 2)]
    peers += [(row, partner)]
    for peer in peers:
        pl.semaphore_signal(barrier, inc=1, device_id=peer, device_id_type=pl.DeviceIdType.MESH)
    pl.semaphore_wait(barrier, len(peers))

    left_copies = [
        remote(left.at[at_row(step)], basis.at[rows_of(row), lanes_of(blk)], at_row(step), blk)
        for step in range(1, nrow)
    ]
    side, across = row + 1 - 2 * lax.rem(row, 2), lax.rem(row + 2, nrow)
    right_copies = [remote(right, right_place(row), peer, blk) for peer in (side, across)]
    grad_copies = [
        remote(
            grad.at[at_row(step)], gathered.at[rows_of(row), pl.ds(0, cols)], at_row(step), blk
        )
        for step in range(1, nrow)
    ]
    load_left.wait()
    for copy in left_copies:
        copy.wait_recv()
    own_lanes = basis.at[:, lanes_of(blk)]
    spread_copies = [
        remote(own_lanes, own_lanes, row, at_blk(step)) for step in range(1, nblk // 2)
    ]
    share_copies = [remote(own_lanes, own_lanes, row, partner)]

    load_grad.wait()
    load_avg.wait()
    for step in list(range(1, nrow)) + [0]:
        index = at_row(step)
        moment = momentum_decay * avg_own[index] + (1.0 - momentum_decay) * grad_own[
            index
        ].astype(jnp.float32)
        moment_out[index] = moment
        if step == 0:
            gathered[rows_of(row), cols:] = moment.astype(jnp.bfloat16)
        else:
            moment_half[index] = moment.astype(jnp.bfloat16)

    depth = cols // 2
    right_copies[0].wait_recv()
    first_half = right_place(side).at[pl.ds(0, depth)]
    forward_copies = [remote(first_half, first_half, across, blk)]
    right_copies[1].wait_recv()
    second_half = right_place(across).at[pl.ds(depth, depth)]
    forward_copies.append(remote(second_half, second_half, side, blk))

    moment_copies = []
    for step in range(1, nrow):
        index = at_row(step)
        moment_copies.append(
            remote(
                moment_half.at[index], gathered.at[rows_of(row), pl.ds(cols, cols)], index, blk
            )
        )

    load_sq.wait()
    for step in list(range(1, nrow)) + [0]:
        index = at_row(step)
        value = sq_own[index].astype(jnp.bfloat16)
        if step == 0:
            sq_all[rows_of(row), :] = value
        else:
            sq_half[index] = value

    load_right.wait()
    for copy in forward_copies:
        copy.wait_recv()
    turn_copy = remote(turn.at[1], turn_other, row, partner)

    load_block.wait()
    for copy in grad_copies:
        copy.wait_recv()

    sq_copies = []
    for step in range(1, nrow):
        index = at_row(step)
        sq_copies.append(remote(sq_half.at[index], sq_all.at[rows_of(row), :], index, blk))

    for step in range(1, nblk // 2):
        spread_copies[step - 1].wait_recv()
        lanes = basis.at[:, lanes_of(at_blk(nblk // 2 - step))]
        share_copies.append(remote(lanes, lanes, row, partner))
    for copy in share_copies:
        copy.wait_recv()

    def turn_left(start):
        copies = []
        for index in range(nrow):
            part = pl.ds(index * brows, brows)
            place = (part, pl.ds(start, cols))
            turned[place] = lax.dot_general(
                basis[:, part],
                gathered[:, pl.ds(start, cols)],
                (((0,), (0,)), ((), ())),
                preferred_element_type=jnp.float32,
            ).astype(jnp.bfloat16)
            copies.append(remote(turned.at[place], turned_other.at[place], row, partner))
        return copies

    def turn_right(part, start):
        place = (part, pl.ds(start, cols))
        term = jnp.dot(turned[place], turn[0], preferred_element_type=jnp.float32)
        return term + jnp.dot(
            turned_other[place], turn_other[...], preferred_element_type=jnp.float32
        )

    turned_copies = turn_left(0)
    turn_copy.wait_recv()
    for copy in turned_copies:
        copy.wait_recv()
    order = list(range(1, nrow)) + [0]
    for step in order:
        part = rows_of(at_row(step))
        grad_term = turn_right(part, 0)
        grad_rot[part, :] = grad_term
        rot_half[part, :] = grad_term.astype(jnp.bfloat16)
    rot_local = local(rot_half.at[rows_of(row), :], rot_out.at[row])

    for copy in moment_copies:
        copy.wait_recv()
    later_copies = turn_left(cols)
    for copy in later_copies:
        copy.wait_recv()
    for step in order:
        part = rows_of(at_row(step))
        moment_rot[part, :] = turn_right(part, cols)

    rot_copies = []

    def send_rot():
        for step in range(1, nrow):
            index = at_row(step)
            rot_copies.append(remote(rot_half.at[rows_of(index), :], rot_out.at[row], index, blk))

    direction_copies = []
    for step in range(nrow):
        part = rows_of(at_row(nrow - step))
        if step:
            sq_copies[step - 1].wait_recv()
        if step == 1:
            send_rot()
        rotated = grad_rot[part, :]
        variance = (
            variance_decay * sq_all[part, :].astype(jnp.float32)
            + (1.0 - variance_decay) * rotated * rotated
        )
        direction[part, :] = (
            moment_rot[part, :] / (jnp.sqrt(variance) + epsilon_value)
        ).astype(jnp.bfloat16)
        direction_copies.append(
            remote(direction.at[part, :], direction_other.at[part, :], row, partner)
        )

    contract = (((1,), (1,)), ((), ()))
    for step in range(nrow):
        part = rows_of(at_row(nrow - step))
        direction_copies[step].wait_recv()
        term = lax.dot_general(
            direction[part, :], turn[0], contract, preferred_element_type=jnp.float32
        )
        term += lax.dot_general(
            direction_other[part, :], turn[1], contract, preferred_element_type=jnp.float32
        )
        back[part, :] = term.astype(jnp.bfloat16)

    update_copies = []
    for step in order:
        index = at_row(step)
        part = rows_of(index)
        update[part, :] = jnp.dot(
            basis[part, :], back[...], preferred_element_type=jnp.float32
        ).astype(jnp.bfloat16)
        if step == 0:
            update_local = local(update.at[part, :], update_out.at[row])
        else:
            update_copies.append(remote(update.at[part, :], update_out.at[row], index, blk))

    rot_local.wait()
    for step in range(nrow):
        index = at_row(nrow - step)
        if step:
            rot_copies[step - 1].wait_recv()
        rotated = rot_out[index].astype(jnp.float32)
        variance_out[index] = (
            variance_decay * sq_own[index] + (1.0 - variance_decay) * rotated * rotated
        )
    update_local.wait()
    for copy in update_copies:
        copy.wait_recv()
    for copy in (
        left_copies
        + grad_copies
        + moment_copies
        + right_copies
        + forward_copies
        + spread_copies
        + share_copies
        + sq_copies
        + [turn_copy]
        + turned_copies
        + later_copies
        + rot_copies
        + direction_copies
        + update_copies
    ):
        copy.wait_send()


def fast_body(grad, exp_avg, exp_avg_sq, left_basis, right_basis):
    blocks, brows, cols = grad.shape
    nrow, nblk = lax.axis_size("row"), lax.axis_size("blk")
    size = nrow * brows
    half, full = jnp.bfloat16, jnp.float32
    vmem = pltpu.VMEM
    remote_count = 6 * (nrow - 1) + 4 + 2 * (nblk // 2 - 1) + 2 + 3 * nrow
    return pl.pallas_call(
        functools.partial(kernel, nrow, nblk),
        out_shape=[vmem(grad.shape, half), vmem(grad.shape, full), vmem(grad.shape, full)],
        in_specs=[pl.BlockSpec(memory_space=pl.ANY)] * 5,
        out_specs=[pl.BlockSpec(memory_space=vmem)] * 3,
        scratch_shapes=[
            vmem(grad.shape, half),
            vmem(grad.shape, half),
            vmem(grad.shape, full),
            vmem(grad.shape, full),
            vmem(grad.shape, half),
            vmem(grad.shape, half),
            vmem((size, 2 * cols), half),
            vmem((size, cols), half),
            vmem((size, size), half),
            vmem((2, cols, cols), half),
            vmem((cols, cols), half),
            vmem((size, 2 * cols), half),
            vmem((size, 2 * cols), half),
            vmem((size, cols), full),
            vmem((size, cols), full),
            vmem((size, cols), half),
            vmem((size, cols), half),
            vmem((size, cols), half),
            vmem((size, cols), half),
            vmem((size, cols), half),
            pltpu.SemaphoreType.DMA((remote_count,)),
            pltpu.SemaphoreType.DMA((remote_count,)),
            pltpu.SemaphoreType.DMA((8,)),
        ],
        compiler_params=pltpu.CompilerParams(
            collective_id=0, has_side_effects=True, vmem_limit_bytes=56 * 2**20
        ),
        cost_estimate=pl.CostEstimate(
            flops=12 * size * size * cols, bytes_accessed=16 * size * cols, transcendentals=0
        ),
    )(grad, exp_avg, exp_avg_sq, left_basis, right_basis)

def body(grad, exp_avg, exp_avg_sq, left_basis, right_basis):
    blocks, brows, cols = grad.shape
    nrow, nblk = lax.axis_size("row"), lax.axis_size("blk")
    size = nrow * brows
    fits = (
        blocks == nrow
        and nrow == 4
        and nblk * left_basis.shape[2] == size
        and size == 2 * cols
        and left_basis.shape[2] % 128 == 0
        and right_basis.shape[0] == cols
        and right_basis.shape[1] * nrow == size
        and right_basis.shape[1] % 128 == 0
        and brows % 128 == 0
    )
    run = fast_body if fits else general_body
    return run(grad, exp_avg, exp_avg_sq, left_basis, right_basis)


def solution(mesh):
    in_specs = (
        P(None, "row", "blk"),
        P(None, "row", "blk"),
        P(None, "row", "blk"),
        P(None, "row", "blk"),
        P("blk", "row"),
    )
    out_specs = (P(None, "row", "blk"), P(None, "row", "blk"), P(None, "row", "blk"))
    return jax.shard_map(body, mesh=mesh, in_specs=in_specs, out_specs=out_specs, check_vma=False)
```
